32 devices in a mesh: ep: 16 (over z, x, core), tp: 2 (over y).
Axes of the slice: x: 2, y: 2, z: 4, core: 2. Of those that a mesh axis runs over, the one named last changes fastest.
Arguments:
- residual_in: bfloat16 [3072, 2048], P('ep'), may hold values from -6 to 6
- shortcut: bfloat16 [3072, 2048], P('ep'), may hold values from -6 to 6
- attn_gain: float32 [2048], replicated, may hold values from 0.25 to 1.75
- moe_gain: float32 [2048], replicated, may hold values from 0.25 to 1.75
- query_weight: bfloat16 [2048, 4096], P('ep', 'tp')
- key_value: bfloat16 [2048, 1024], P('ep')
- output_weight: bfloat16 [2048, 4096], P('ep', 'tp'), may hold values from -0.09375 to 0.09375
- query_gain: float32 [128], replicated, may hold values from 0.5 to 5
- key_gain: float32 [128], replicated, may hold values from 0.5 to 5
- router_weight: bfloat16 [16, 2048], replicated, may hold values from -0.125 to 0.125
- expert_ids: int32 [3072, 8], P('ep'), may hold values from 0 to 15, all different within a row; in each aligned block of 192 rows (0 to 191, 192 to 383, ...) at most 120 rows name the same one
- gate_up_weight: bfloat16 [32, 2048, 1536], P(('ep', 'tp')), may hold values from -0.125 to 0.125
- down_weight: bfloat16 [32, 768, 2048], P(('ep', 'tp')), may hold values from -0.15625 to 0.15625
Outputs:
- layer_out: bfloat16 [3072, 2048], P('ep')
The draws below stay inside these ranges and needn't reach their ends.
Inputs may be any that keep to these rules, and one draw needn't show every extreme that they name: `expert_ids`: each row names 8 different experts. Among the 192 rows of one sequence no expert is named by more than 120 rows, a bound that some block reaches.
All inputs are finite; a program needn't handle non-finite values.
Results may differ from the reference program's by a relative error of at most 0.009.
Values may be sent and summed in bfloat16 or wider, within the bound.
A program may use at most 128 MiB of HBM per device.

```python
import math
import jax
import jax.numpy as jnp
import numpy as np
from jax import lax

D = 2048
HD = 128
QH = 32
KVH = 4
FF = 1536
TOPK = 8
ROWS = 192
EXPERTS = 16
TOKENS = 3072
QH_DEV = 16
GROUP = 8
FF_DEV = 768
CAP = 120
N_EP = 16
N_TP = 2


def common_base(key):
    return jax.random.normal(jax.random.fold_in(key, 97), (D, KVH * HD), jnp.float32)


def draw_query_weight(key, part):
    key = jax.random.fold_in(key, 11)
    noise = jax.random.normal(key, (D, QH * HD), jnp.float32)
    mixed = noise
    return (mixed * D ** (-0.5)).astype(jnp.bfloat16)


def draw_key_value(key, part):
    base = common_base(key)
    key = jax.random.fold_in(key, 23)
    values = jax.random.normal(key, (D, KVH * HD), jnp.float32)
    return (jnp.concatenate([base, values], 1) * D ** (-0.5)).astype(jnp.bfloat16)


def draw_query_gain(key, part):
    key = jax.random.fold_in(key, 31)
    return jax.random.uniform(key, (HD,), jnp.float32, 0.5, 1.5)


def draw_key_gain(key, part):
    key = jax.random.fold_in(key, 37)
    return jax.random.uniform(key, (HD,), jnp.float32, 0.5, 1.5)


def level_of(key, dims, split, least, top_value):
    level = 1.0
    for axis_at, blocks in split:
        steps = jax.random.uniform(jax.random.fold_in(jax.random.fold_in(key, 6), axis_at), (blocks,), jnp.float32, least / len(split), top_value / len(split))
        level = level * jnp.repeat(jnp.exp(steps), dims[axis_at] // blocks).reshape((-1,) + (1,) * (len(dims) - 1 - axis_at))
    return level


def routed_block(key, own, number, rows, amount, top, limit, skew):
    sequence = jax.random.permutation(key, amount)
    packed, usual = portions_of(amount, rows * top, limit, skew, True), portions_of(amount, rows * top, limit, skew, False)
    places = jnp.arange(amount)

    def named(lengths, rotation):
        used = int((lengths > 0).sum())
        fixed = max(1, used // 4)
        moved = fixed + (places - fixed + rotation * (used - fixed)) % max(1, amount - fixed)
        return jnp.zeros((amount,), jnp.int32).at[sequence[jnp.where(places < fixed, places, moved)]].set(jnp.asarray(lengths, jnp.int32))

    lengths = jnp.where(number % 4 == 0, named(packed, number // 4), named(usual, number - number // 4 - 1))
    mixed = jax.random.permutation(jax.random.fold_in(own, 3), amount)
    donor, receiver = mixed[0:amount // 2 * 2:2], mixed[1:amount // 2 * 2:2]
    margin = jnp.minimum(lengths[donor] - 1, limit - lengths[receiver]) // 2
    margin = jnp.where((donor == sequence[0]) | (receiver == sequence[0]) | (lengths[receiver] == 0), 0, jnp.maximum(margin, 0))
    moved = jax.random.randint(jax.random.fold_in(own, 4), (amount // 2,), 0, 1 << 20) % (margin + 1)
    lengths = lengths.at[donor].add(-moved).at[receiver].add(moved)
    items = jnp.searchsorted(jnp.cumsum(lengths), jnp.arange(rows * top), side="right").astype(jnp.int32)
    table = items.reshape(top, rows).T
    table = table[jax.random.permutation(jax.random.fold_in(own, 1), rows)]
    rotation = jax.random.randint(jax.random.fold_in(own, 2), (rows, 1), 0, top)
    return jnp.take_along_axis(table, (jnp.arange(top)[None, :] + rotation) % top, axis=1)


def portions_of(count, total, reach, lean, full):
    weights = [(1 << 20) // math.isqrt(standing ** lean) + 1 for standing in range(1, count + 1)]
    largest = reach if full else min(reach, max(-(-total // count), total * weights[0] // sum(weights)))
    least = 1 if total - largest >= count - 1 else 0
    holding, spare = [largest] + [least] * (count - 1), total - largest - least * (count - 1)
    while spare > 0:
        free = [i for i in range(1, count) if holding[i] < largest] or [i for i in range(1, count) if holding[i] < reach]
        whole, left = sum([weights[i] for i in free]), spare
        for i in free:
            more = min(reach - holding[i], max(1, left * weights[i] // whole), spare)
            holding[i] = holding[i] + more
            spare = spare - more
    return np.array(holding)


def bell_draw(rng, shape, width, bound, split=(), kind=jnp.bfloat16):
    array = width * jax.random.normal(rng, shape, jnp.float32)
    if split:
        array = array * level_of(rng, shape, split, -0.22, 0.18)
    return jnp.clip(array, -bound, bound).astype(kind)


def setup_inputs(seed: int = 0) -> dict:
    streams_of = jax.random.split(jax.random.key(seed), 14)
    residual_in = bell_draw(streams_of[0], (TOKENS, D), 1.0, 6.0, ((0, 16),))
    shortcut = bell_draw(streams_of[1], (TOKENS, D), 1.0, 6.0, ((0, 16),))
    attn_gain = jnp.clip(1.0 + 0.15 * jax.random.normal(streams_of[2], (D,), jnp.float32), 0.25, 1.75)
    moe_gain = jnp.clip(1.0 + 0.15 * jax.random.normal(streams_of[3], (D,), jnp.float32), 0.25, 1.75)
    query_weight = draw_query_weight(jax.random.fold_in(streams_of[13], 71), 0)
    key_value = draw_key_value(jax.random.fold_in(streams_of[13], 71), 0)
    output_weight = bell_draw(streams_of[6], (D, QH * HD), (QH * HD) ** -0.5, 0.09375, ((0, 16), (1, 2)))
    query_gain = draw_query_gain(jax.random.fold_in(streams_of[13], 71), 0)
    key_gain = draw_key_gain(jax.random.fold_in(streams_of[13], 71), 0)
    router_weight = bell_draw(streams_of[9], (EXPERTS, D), D ** -0.5, 0.125)
    expert_ids_keys = jax.random.split(jax.random.fold_in(streams_of[10], 1), TOKENS // ROWS)
    expert_ids_turns = jax.random.permutation(jax.random.fold_in(streams_of[10], 3), TOKENS // ROWS)
    expert_ids = jax.vmap(lambda own, number: routed_block(jax.random.fold_in(streams_of[10], 2), own, number, ROWS, EXPERTS, TOPK, CAP, 2))(expert_ids_keys, expert_ids_turns).reshape((TOKENS, TOPK))
    gate_up_weight = bell_draw(streams_of[11], (2 * EXPERTS, D, 2 * FF_DEV), D ** -0.5, 0.125, ((0, 32),))
    down_weight = bell_draw(streams_of[12], (2 * EXPERTS, FF_DEV, D), FF ** -0.5, 0.15625, ((0, 32),))
    return dict(residual_in=residual_in, shortcut=shortcut, attn_gain=attn_gain, moe_gain=moe_gain, query_weight=query_weight, key_value=key_value, output_weight=output_weight, query_gain=query_gain, key_gain=key_gain, router_weight=router_weight, expert_ids=expert_ids, gate_up_weight=gate_up_weight, down_weight=down_weight)


EPS = 1e-06
ROPE_BASE = 1000000.0

def norm_rows(values, gain):
    wide = values.astype(jnp.float32)
    return wide * lax.rsqrt(lax.optimization_barrier(jnp.mean(wide * wide, -1, keepdims=True)) + EPS) * gain.astype(jnp.float32)

def rotary(values):
    length = values.shape[0]
    half = values.shape[-1] // 2
    position = jnp.arange(length, dtype=jnp.float32)
    freq = ROPE_BASE ** (-jnp.arange(half, dtype=jnp.float32) * 2.0 / values.shape[-1])
    angle = position[:, None] * freq[None, :]
    cosine = jnp.cos(angle)[:, None, :]
    sine = jnp.sin(angle)[:, None, :]
    first = values[..., :half]
    second = values[..., half:]
    return jnp.concatenate([first * cosine - second * sine, second * cosine + first * sine], -1)

def reference(residual_in, shortcut, attn_gain, moe_gain, query_weight, key_value, output_weight, query_gain, key_gain, router_weight, expert_ids, gate_up_weight, down_weight):
    attn_rows = norm_rows(residual_in, attn_gain).astype(jnp.bfloat16)
    moe_rows = norm_rows(shortcut, moe_gain).astype(jnp.bfloat16)

    def one_sequence(rows):
        query = jnp.dot(rows, query_weight, preferred_element_type=jnp.float32).reshape(ROWS, QH, HD)
        query = rotary(norm_rows(query, query_gain)).astype(jnp.bfloat16).reshape(ROWS, KVH, GROUP, HD)
        keyval = jnp.dot(rows, key_value, preferred_element_type=jnp.float32).reshape(ROWS, 2, KVH, HD)
        keys = rotary(norm_rows(keyval[:, 0], key_gain)).astype(jnp.bfloat16)
        values = keyval[:, 1].astype(jnp.bfloat16)
        logits = jnp.einsum('sgjd,tgd->gjst', query.astype(jnp.float32), keys.astype(jnp.float32)) * HD ** (-0.5)
        causal = jnp.arange(ROWS)[:, None] >= jnp.arange(ROWS)[None, :]
        logits = jnp.where(causal, logits, -1e+30)
        peak = lax.optimization_barrier(jnp.max(logits, -1, keepdims=True))
        expo = jnp.exp(logits - peak)
        probs = (expo / lax.optimization_barrier(jnp.sum(expo, -1, keepdims=True))).astype(jnp.bfloat16)
        attended = jnp.einsum('gjst,tgd->sgjd', probs.astype(jnp.float32), values.astype(jnp.float32))
        attended = attended.astype(jnp.bfloat16).reshape(ROWS, N_TP, QH_DEV * HD)
        out_split = output_weight.reshape(D, N_TP, QH_DEV * HD)
        total = jnp.zeros((ROWS, D), jnp.float32)
        for index in range(N_TP):
            part = jnp.dot(attended[:, index], out_split[:, index].T, preferred_element_type=jnp.float32)
            total = total + lax.optimization_barrier(part.astype(jnp.bfloat16)).astype(jnp.float32)
        return total
    attention = lax.map(one_sequence, attn_rows.reshape(N_EP, ROWS, D)).reshape(TOKENS, D)
    logits_router = jnp.dot(moe_rows, router_weight.T, preferred_element_type=jnp.float32)
    chosen = jnp.take_along_axis(logits_router, expert_ids, axis=1)
    scores = jax.nn.sigmoid(chosen)
    gates = (scores / lax.optimization_barrier(jnp.sum(scores, 1, keepdims=True))).astype(jnp.bfloat16)
    hits = (expert_ids[:, :, None] == jnp.arange(EXPERTS, dtype=jnp.int32)[None, None, :]).astype(jnp.int32)
    per_row = lax.optimization_barrier(jnp.sum(hits, 1)).astype(jnp.int32).reshape(TOKENS // ROWS, ROWS, EXPERTS)
    earlier = (jnp.cumsum(per_row, 1).astype(jnp.int32) - per_row).reshape(TOKENS, EXPERTS)
    slot = jnp.take_along_axis(earlier, expert_ids, axis=1).astype(jnp.int32)
    device = (jnp.arange(TOKENS, dtype=jnp.int32) // ROWS)[:, None]
    place = (device * CAP + slot).astype(jnp.int32)
    buffer_rows = TOKENS // ROWS * CAP
    gate_up_split = gate_up_weight.reshape(EXPERTS, 2, D, 2 * FF_DEV)
    down_split = down_weight.reshape(EXPERTS, 2, FF_DEV, D)

    def one_expert(total, inputs):
        index, gate_up, down = inputs
        hit = expert_ids == index
        any_hit = jnp.any(hit, 1)
        summed_place = lax.optimization_barrier(jnp.sum(jnp.where(hit, place, 0), 1)).astype(jnp.int32)
        row_place = jnp.where(any_hit, summed_place, buffer_rows).astype(jnp.int32)
        buffer = jnp.zeros((buffer_rows, D), jnp.bfloat16).at[row_place].set(moe_rows, mode='drop')
        summed = jnp.zeros((buffer_rows, D), jnp.float32)
        for half in range(2):
            paired = jnp.dot(buffer, gate_up[half], preferred_element_type=jnp.float32)
            hidden = (jax.nn.silu(paired[:, :FF_DEV]) * paired[:, FF_DEV:]).astype(jnp.bfloat16)
            summed = summed + jnp.dot(hidden, down[half], preferred_element_type=jnp.float32)
        expert_out = summed.astype(jnp.bfloat16).astype(jnp.float32)
        weight = lax.optimization_barrier(jnp.sum(jnp.where(hit, gates.astype(jnp.float32), 0.0), 1))
        picked = expert_out[jnp.minimum(row_place, buffer_rows - 1)]
        return (total + weight[:, None] * picked, None)
    moe_out, _ = lax.scan(one_expert, jnp.zeros((TOKENS, D), jnp.float32), (jnp.arange(EXPERTS, dtype=jnp.int32), gate_up_split, down_split))
    return (residual_in.astype(jnp.float32) + attention + moe_out).astype(jnp.bfloat16)
```

```python
import jax
import jax.numpy as jnp
from jax.experimental import pallas as pl
from jax.experimental.pallas import tpu as pltpu
from jax import lax
from jax.sharding import PartitionSpec as P

HD = 128
QH = 32
KVH = 4
TOPK = 8


EPS = 1e-06
ROPE_BASE = 1000000.0


def from_partner(value, axis, apart):
    mask = 2**apart
    pairs = [(source, source ^ mask) for source in range(lax.axis_size(axis))]
    return lax.ppermute(value, axis, pairs)


def norm_rows(values, gain):
    wide = values.astype(jnp.float32)
    return wide * lax.rsqrt(jnp.mean(wide * wide, -1, keepdims=True) + EPS) * gain


def rotary(values):
    length = values.shape[0]
    half = values.shape[-1] // 2
    position = jnp.arange(length, dtype=jnp.float32)
    freq = ROPE_BASE ** (-jnp.arange(half, dtype=jnp.float32) * 2.0 / values.shape[-1])
    angle = position[:, None] * freq[None, :]
    cosine = jnp.cos(angle)[:, None, :]
    sine = jnp.sin(angle)[:, None, :]
    first = values[..., :half]
    second = values[..., half:]
    return jnp.concatenate([first * cosine - second * sine, second * cosine + first * sine], -1)


def capacity_of(rows, experts):
    return max(2, 5 * rows * TOPK // (4 * experts))


def attend(query, keyval, query_gain, key_gain, kv_count):
    seq = query.shape[0]
    query = rotary(norm_rows(query.reshape(seq, -1, HD), query_gain)).astype(jnp.bfloat16)
    heads = query.shape[1]
    query = query.reshape(seq, kv_count, heads // kv_count, HD)
    keyval = keyval.reshape(seq, 2, kv_count, HD)
    keys = rotary(norm_rows(keyval[:, 0], key_gain)).astype(jnp.bfloat16)
    values = keyval[:, 1].astype(jnp.bfloat16)
    logits = jnp.einsum("sgjd,tgd->gjst", query, keys, preferred_element_type=jnp.float32) * HD ** (
        -0.5
    )
    causal = jnp.arange(seq)[:, None] >= jnp.arange(seq)[None, :]
    logits = jnp.where(causal, logits, -1e30)
    peak = jnp.max(logits, -1, keepdims=True)
    expo = jnp.exp(logits - peak)
    probs = (expo / jnp.sum(expo, -1, keepdims=True)).astype(jnp.bfloat16)
    attended = jnp.einsum("gjst,tgd->sgjd", probs, values, preferred_element_type=jnp.float32)
    return attended.astype(jnp.bfloat16).reshape(seq, heads * HD)


def project_out(attended, weight):
    return lax.dot_general(
        attended, weight, (((1,), (1,)), ((), ())), preferred_element_type=jnp.float32
    )


def weights_first(
    residual_in,
    shortcut,
    attn_gain,
    moe_gain,
    query_weight,
    key_value,
    output_weight,
    query_gain,
    key_gain,
    router_weight,
    expert_ids,
    gate_up_weight,
    down_weight,
):
    n_ep = lax.axis_size("ep")
    n_tp = lax.axis_size("tp")
    rank = lax.axis_index("tp")
    pairs = n_tp // 2
    group_id = rank // 2
    side = rank % 2
    rows, d_model = residual_in.shape
    half_width = d_model // 2
    experts = router_weight.shape[0]
    capacity = capacity_of(rows, experts)
    ff_dev = down_weight.shape[1]
    qh_dev = query_weight.shape[1] // HD
    group = QH // KVH
    kv_count = max(1, qh_dev // group)
    kv_start = rank * qh_dev // group
    attn_rows = norm_rows(residual_in, attn_gain).astype(jnp.bfloat16)
    moe_rows = norm_rows(shortcut, moe_gain).astype(jnp.bfloat16)
    logits_router = lax.dot_general(
        moe_rows, router_weight, (((1,), (1,)), ((), ())), preferred_element_type=jnp.float32
    )
    hits = (expert_ids[:, :, None] == jnp.arange(experts, dtype=jnp.int32)[None, None, :]).astype(
        jnp.float32
    )
    chosen = jnp.sum(hits * logits_router[:, None, :], -1)
    scores = jax.nn.sigmoid(chosen)
    gates = (scores / jnp.sum(scores, 1, keepdims=True)).astype(jnp.bfloat16)
    per_row = jnp.sum(hits, 1).astype(jnp.bfloat16)
    lower = (jnp.arange(rows)[:, None] > jnp.arange(rows)[None, :]).astype(jnp.bfloat16)
    earlier = jnp.dot(lower, per_row, preferred_element_type=jnp.float32)
    slot = jnp.sum(hits * earlier[:, None, :], -1)
    mine = expert_ids % pairs == group_id
    target = (expert_ids // pairs).astype(jnp.float32) * capacity + slot
    target = jnp.where(mine, target, -1.0)
    places = jnp.arange(n_ep * capacity, dtype=jnp.float32)
    match = (target[:, :, None] == places[None, None, :]).astype(jnp.float32)
    dispatch_map = jnp.sum(match, 1).astype(jnp.bfloat16)
    combine = jnp.sum(match * gates.astype(jnp.float32)[:, :, None], 1).astype(jnp.bfloat16)
    outgoing = lax.dot_general(
        dispatch_map, moe_rows, (((0,), (0,)), ((), ())), preferred_element_type=jnp.float32
    ).astype(jnp.bfloat16)
    outgoing = outgoing.reshape(n_ep, capacity, d_model)
    arrived = lax.all_to_all(outgoing, "ep", split_axis=0, concat_axis=0, tiled=True)
    paired = jnp.einsum(
        "ack,kf->acf", arrived, gate_up_weight[0], preferred_element_type=jnp.float32
    )
    hidden = (jax.nn.silu(paired[..., :ff_dev]) * paired[..., ff_dev:]).astype(jnp.bfloat16)
    partial_sum = jnp.einsum(
        "acf,fk->ack", hidden, down_weight[0], preferred_element_type=jnp.float32
    )
    kept = lax.dynamic_slice_in_dim(partial_sum, side * half_width, half_width, 2)
    handed = lax.dynamic_slice_in_dim(partial_sum, (1 - side) * half_width, half_width, 2)
    received = from_partner(handed.astype(jnp.bfloat16), "tp", 0).astype(handed.dtype)
    expert_out = (kept + received).astype(jnp.bfloat16)
    returned = lax.all_to_all(expert_out, "ep", split_axis=0, concat_axis=0, tiled=True).reshape(
        -1, half_width
    )
    moe_cols = jnp.dot(combine, returned, preferred_element_type=jnp.float32)
    blank = jnp.zeros_like(moe_cols)
    moe_full = jnp.where(
        side == 0, jnp.concatenate([moe_cols, blank], 1), jnp.concatenate([blank, moe_cols], 1)
    )
    local_rows = key_value.shape[0]
    local_kv = lax.dynamic_slice_in_dim(
        key_value.reshape(local_rows, 2, KVH, HD), kv_start, kv_count, 2
    )
    local_kv = local_kv.reshape(local_rows, 2 * kv_count * HD)
    full_query, full_kv, full_out = (
        lax.all_gather(query_weight, "ep", axis=0, tiled=True),
        lax.all_gather(local_kv, "ep", axis=0, tiled=True),
        lax.all_gather(output_weight, "ep", axis=0, tiled=True),
    )
    query = jnp.dot(attn_rows, full_query, preferred_element_type=jnp.float32)
    keyval = jnp.dot(attn_rows, full_kv, preferred_element_type=jnp.float32)
    attended = attend(query, keyval, query_gain, key_gain, kv_count)
    attn_terms = project_out(attended, full_out)
    attn_part = attn_terms.astype(jnp.bfloat16).astype(jnp.float32)
    total = attn_part + moe_full
    summed = lax.psum(total, "tp")
    return (residual_in.astype(jnp.float32) + summed).astype(jnp.bfloat16)


def rotary_tables(length, width):
    half = width // 2
    position = jnp.arange(length, dtype=jnp.float32)
    freq = ROPE_BASE ** (-jnp.arange(half, dtype=jnp.float32) * 2.0 / width)
    angle = position[:, None] * freq[None, :]
    cosine, sine = jnp.cos(angle), jnp.sin(angle)
    return jnp.concatenate([cosine, cosine], 1), jnp.concatenate([-sine, sine], 1)


def spread_gates(moe_rows, router_weight, expert_ids):
    experts = router_weight.shape[0]
    logits = lax.dot_general(
        moe_rows, router_weight, (((1,), (1,)), ((), ())), preferred_element_type=jnp.float32
    )
    hits = jnp.any(
        expert_ids[:, :, None] == jnp.arange(experts, dtype=jnp.int32)[None, None, :], 1
    )
    scores = jnp.where(hits, jax.nn.sigmoid(logits), 0.0)
    return scores / jnp.sum(scores, 1, keepdims=True)


def rotated_norm(values, gain, cosine, sine):
    wide = values * lax.rsqrt(jnp.mean(values * values, -1, keepdims=True) + EPS) * gain
    return (wide * cosine + pltpu.roll(wide, HD // 2, 1) * sine).astype(jnp.bfloat16)


def attend_head(qkv, query_gain, key_gain, cosine, sine):
    seq = qkv.shape[0]
    query = rotated_norm(qkv[:, :HD], query_gain, cosine, sine)
    keys = rotated_norm(qkv[:, HD : 2 * HD], key_gain, cosine, sine)
    values = qkv[:, 2 * HD :].astype(jnp.bfloat16)
    logits = lax.dot_general(
        query, keys, (((1,), (1,)), ((), ())), preferred_element_type=jnp.float32
    ) * HD ** (-0.5)
    below = lax.broadcasted_iota(jnp.int32, (seq, seq), 0) >= lax.broadcasted_iota(
        jnp.int32, (seq, seq), 1
    )
    logits = jnp.where(below, logits, -1e30)
    expo = jnp.exp(logits - jnp.max(logits, -1, keepdims=True))
    probs = (expo / jnp.sum(expo, -1, keepdims=True)).astype(jnp.bfloat16)
    return jnp.dot(probs, values, preferred_element_type=jnp.float32).astype(jnp.bfloat16)


def heads_and_expert(
    seq, attn_ref, moe_ref, qkv_ref, out_w_ref, up_ref, down_ref, qg_ref, kg_ref, cos_ref, sin_ref,
    out_ref,
):
    d_model = attn_ref.shape[1]
    ff_dev = down_ref.shape[0]
    expert = lax.axis_index("ep")
    qkv = jnp.dot(attn_ref[...], qkv_ref[...], preferred_element_type=jnp.float32)
    parts = [
        attend_head(qkv[at : at + seq], qg_ref[...], kg_ref[...], cos_ref[...], sin_ref[...])
        for at in range(0, qkv.shape[0], seq)
    ]
    attended = jnp.concatenate(parts, 0)
    gates = moe_ref[:, d_model:].astype(jnp.float32)
    lane = lax.broadcasted_iota(jnp.int32, gates.shape, 1)
    gate = jnp.sum(jnp.where(lane == expert, gates, 0.0), 1, keepdims=True)
    paired = jnp.dot(moe_ref[:, :d_model], up_ref[...], preferred_element_type=jnp.float32)
    front, back = paired[:, :ff_dev], paired[:, ff_dev:]
    hidden = (front / (1.0 + jnp.exp(-front)) * back * gate).astype(jnp.bfloat16)
    total = jnp.dot(hidden, down_ref[...], preferred_element_type=jnp.float32)
    total += jnp.dot(attended, out_w_ref[...], preferred_element_type=jnp.float32)
    out_ref[...] = total.astype(out_ref.dtype)


def rows_first(
    residual_in,
    shortcut,
    attn_gain,
    moe_gain,
    query_weight,
    key_value,
    output_weight,
    query_gain,
    key_gain,
    router_weight,
    expert_ids,
    gate_up_weight,
    down_weight,
):
    n_ep = lax.axis_size("ep")
    n_tp = lax.axis_size("tp")
    me, rank = lax.axis_index("ep"), lax.axis_index("tp")
    rows, d_model = residual_in.shape
    share = rows // n_tp
    depth = key_value.shape[0]
    residual = lax.dynamic_slice_in_dim(residual_in, rank * share, share, 0)
    attn_rows = norm_rows(residual, attn_gain).astype(jnp.bfloat16)
    moe_rows = norm_rows(
        lax.dynamic_slice_in_dim(shortcut, rank * share, share, 0), moe_gain
    ).astype(jnp.bfloat16)
    ids = lax.dynamic_slice_in_dim(expert_ids, rank * share, share, 0)
    gates = spread_gates(moe_rows, router_weight, ids).astype(jnp.bfloat16)
    gates = jnp.pad(gates, ((0, 0), (0, HD - gates.shape[1])))
    moe_rows = jnp.concatenate([moe_rows, gates], 1)
    all_attn = lax.all_gather(attn_rows, ("ep", "tp"), axis=0, tiled=True)
    all_moe = lax.all_gather(moe_rows, ("ep", "tp"), axis=0, tiled=True)

    kv_count = KVH // n_tp
    kv = lax.dynamic_slice_in_dim(
        key_value.reshape(depth, 2, KVH, HD), rank * kv_count, kv_count, 2
    )
    kv = jnp.repeat(kv, n_ep // kv_count, 2).transpose(0, 2, 1, 3).reshape(depth, n_ep, 2 * HD)
    sent = jnp.concatenate(
        [query_weight.reshape(depth, n_ep, HD), kv, output_weight.reshape(depth, n_ep, HD)], 2
    )
    mine = lax.all_to_all(sent, "ep", split_axis=1, concat_axis=0, tiled=True)
    mine = mine.reshape(d_model, 4 * HD)
    cosine, sine = rotary_tables(rows, HD)
    block = 2 * rows
    whole = lambda *shape: pl.BlockSpec(shape, lambda i: (0,) * len(shape))
    ff_dev = down_weight.shape[1]
    total = n_ep * rows
    partial_sum = pl.pallas_call(
        lambda *refs: heads_and_expert(rows, *refs),
        grid=(total // block,),
        in_specs=[
            pl.BlockSpec((block, d_model), lambda i: (i, 0)),
            pl.BlockSpec((block, d_model + HD), lambda i: (i, 0)),
            whole(d_model, 3 * HD),
            whole(HD, d_model),
            whole(d_model, 2 * ff_dev),
            whole(ff_dev, d_model),
            whole(1, HD),
            whole(1, HD),
            whole(rows, HD),
            whole(rows, HD),
        ],
        out_specs=pl.BlockSpec((block, d_model), lambda i: (i, 0)),
        out_shape=jax.ShapeDtypeStruct((total, d_model), jnp.bfloat16),
        compiler_params=pltpu.CompilerParams(vmem_limit_bytes=56 * 2**20),
        cost_estimate=pl.CostEstimate(
            flops=2 * total * d_model * (3 * ff_dev + 4 * HD),
            bytes_accessed=total * d_model * 6 + 3 * ff_dev * d_model * 2,
            transcendentals=total * ff_dev,
        ),
    )(
        all_attn, all_moe, mine[:, : 3 * HD], mine[:, 3 * HD :].T, gate_up_weight[0],
        down_weight[0], query_gain[None], key_gain[None], cosine, sine,
    )
    summed = lax.psum_scatter(partial_sum, ("ep", "tp"), scatter_dimension=0, tiled=True)
    out = (residual.astype(jnp.float32) + summed.astype(jnp.float32)).astype(jnp.bfloat16)
    return lax.all_gather(out, "tp", axis=0, tiled=True)


def solution(mesh):
    n_ep, n_tp = mesh.shape["ep"], mesh.shape["tp"]
    local = rows_first if n_ep * n_tp == QH and n_tp == 2 else weights_first
    return jax.shard_map(
        local,
        mesh=mesh,
        in_specs=(
            P("ep", None),
            P("ep", None),
            P(),
            P(),
            P("ep", "tp"),
            P("ep", None),
            P("ep", "tp"),
            P(),
            P(),
            P(),
            P("ep", None),
            P(("ep", "tp"), None, None),
            P(("ep", "tp"), None, None),
        ),
        out_specs=P("ep", None),
        check_vma=False,
    )
```

```python
import jax
import jax.numpy as jnp
from jax.experimental import pallas as pl
from jax.experimental.pallas import tpu as pltpu
from jax import lax
from jax.sharding import PartitionSpec as P

HD = 128
QH = 32
KVH = 4
TOPK = 8


EPS = 1e-06
ROPE_BASE = 1000000.0


def from_partner(value, axis, apart):
    mask = 2**apart
    pairs = [(source, source ^ mask) for source in range(lax.axis_size(axis))]
    return lax.ppermute(value, axis, pairs)


def norm_rows(values, gain):
    wide = values.astype(jnp.float32)
    return wide * lax.rsqrt(jnp.mean(wide * wide, -1, keepdims=True) + EPS) * gain


def rotary(values):
    length = values.shape[0]
    half = values.shape[-1] // 2
    position = jnp.arange(length, dtype=jnp.float32)
    freq = ROPE_BASE ** (-jnp.arange(half, dtype=jnp.float32) * 2.0 / values.shape[-1])
    angle = position[:, None] * freq[None, :]
    cosine = jnp.cos(angle)[:, None, :]
    sine = jnp.sin(angle)[:, None, :]
    first = values[..., :half]
    second = values[..., half:]
    return jnp.concatenate([first * cosine - second * sine, second * cosine + first * sine], -1)


def capacity_of(rows, experts):
    return max(2, 5 * rows * TOPK // (4 * experts))


def attend(query, keyval, query_gain, key_gain, kv_count):
    seq = query.shape[0]
    query = rotary(norm_rows(query.reshape(seq, -1, HD), query_gain)).astype(jnp.bfloat16)
    heads = query.shape[1]
    query = query.reshape(seq, kv_count, heads // kv_count, HD)
    keyval = keyval.reshape(seq, 2, kv_count, HD)
    keys = rotary(norm_rows(keyval[:, 0], key_gain)).astype(jnp.bfloat16)
    values = keyval[:, 1].astype(jnp.bfloat16)
    logits = jnp.einsum("sgjd,tgd->gjst", query, keys, preferred_element_type=jnp.float32) * HD ** (
        -0.5
    )
    causal = jnp.arange(seq)[:, None] >= jnp.arange(seq)[None, :]
    logits = jnp.where(causal, logits, -1e30)
    peak = jnp.max(logits, -1, keepdims=True)
    expo = jnp.exp(logits - peak)
    probs = (expo / jnp.sum(expo, -1, keepdims=True)).astype(jnp.bfloat16)
    attended = jnp.einsum("gjst,tgd->sgjd", probs, values, preferred_element_type=jnp.float32)
    return attended.astype(jnp.bfloat16).reshape(seq, heads * HD)


def project_out(attended, weight):
    return lax.dot_general(
        attended, weight, (((1,), (1,)), ((), ())), preferred_element_type=jnp.float32
    )


def weights_first(
    residual_in,
    shortcut,
    attn_gain,
    moe_gain,
    query_weight,
    key_value,
    output_weight,
    query_gain,
    key_gain,
    router_weight,
    expert_ids,
    gate_up_weight,
    down_weight,
):
    n_ep = lax.axis_size("ep")
    n_tp = lax.axis_size("tp")
    rank = lax.axis_index("tp")
    pairs = n_tp // 2
    group_id = rank // 2
    side = rank % 2
    rows, d_model = residual_in.shape
    half_width = d_model // 2
    experts = router_weight.shape[0]
    capacity = capacity_of(rows, experts)
    ff_dev = down_weight.shape[1]
    qh_dev = query_weight.shape[1] // HD
    group = QH // KVH
    kv_count = max(1, qh_dev // group)
    kv_start = rank * qh_dev // group
    attn_rows = norm_rows(residual_in, attn_gain).astype(jnp.bfloat16)
    moe_rows = norm_rows(shortcut, moe_gain).astype(jnp.bfloat16)
    logits_router = lax.dot_general(
        moe_rows, router_weight, (((1,), (1,)), ((), ())), preferred_element_type=jnp.float32
    )
    hits = (expert_ids[:, :, None] == jnp.arange(experts, dtype=jnp.int32)[None, None, :]).astype(
        jnp.float32
    )
    chosen = jnp.sum(hits * logits_router[:, None, :], -1)
    scores = jax.nn.sigmoid(chosen)
    gates = (scores / jnp.sum(scores, 1, keepdims=True)).astype(jnp.bfloat16)
    per_row = jnp.sum(hits, 1).astype(jnp.bfloat16)
    lower = (jnp.arange(rows)[:, None] > jnp.arange(rows)[None, :]).astype(jnp.bfloat16)
    earlier = jnp.dot(lower, per_row, preferred_element_type=jnp.float32)
    slot = jnp.sum(hits * earlier[:, None, :], -1)
    mine = expert_ids % pairs == group_id
    target = (expert_ids // pairs).astype(jnp.float32) * capacity + slot
    target = jnp.where(mine, target, -1.0)
    places = jnp.arange(n_ep * capacity, dtype=jnp.float32)
    match = (target[:, :, None] == places[None, None, :]).astype(jnp.float32)
    dispatch_map = jnp.sum(match, 1).astype(jnp.bfloat16)
    combine = jnp.sum(match * gates.astype(jnp.float32)[:, :, None], 1).astype(jnp.bfloat16)
    outgoing = lax.dot_general(
        dispatch_map, moe_rows, (((0,), (0,)), ((), ())), preferred_element_type=jnp.float32
    ).astype(jnp.bfloat16)
    outgoing = outgoing.reshape(n_ep, capacity, d_model)
    arrived = lax.all_to_all(outgoing, "ep", split_axis=0, concat_axis=0, tiled=True)
    paired = jnp.einsum(
        "ack,kf->acf", arrived, gate_up_weight[0], preferred_element_type=jnp.float32
    )
    hidden = (jax.nn.silu(paired[..., :ff_dev]) * paired[..., ff_dev:]).astype(jnp.bfloat16)
    partial_sum = jnp.einsum(
        "acf,fk->ack", hidden, down_weight[0], preferred_element_type=jnp.float32
    )
    kept = lax.dynamic_slice_in_dim(partial_sum, side * half_width, half_width, 2)
    handed = lax.dynamic_slice_in_dim(partial_sum, (1 - side) * half_width, half_width, 2)
    received = from_partner(handed.astype(jnp.bfloat16), "tp", 0).astype(handed.dtype)
    expert_out = (kept + received).astype(jnp.bfloat16)
    returned = lax.all_to_all(expert_out, "ep", split_axis=0, concat_axis=0, tiled=True).reshape(
        -1, half_width
    )
    moe_cols = jnp.dot(combine, returned, preferred_element_type=jnp.float32)
    blank = jnp.zeros_like(moe_cols)
    moe_full = jnp.where(
        side == 0, jnp.concatenate([moe_cols, blank], 1), jnp.concatenate([blank, moe_cols], 1)
    )
    local_rows = key_value.shape[0]
    local_kv = lax.dynamic_slice_in_dim(
        key_value.reshape(local_rows, 2, KVH, HD), kv_start, kv_count, 2
    )
    local_kv = local_kv.reshape(local_rows, 2 * kv_count * HD)
    full_query, full_kv, full_out = (
        lax.all_gather(query_weight, "ep", axis=0, tiled=True),
        lax.all_gather(local_kv, "ep", axis=0, tiled=True),
        lax.all_gather(output_weight, "ep", axis=0, tiled=True),
    )
    query = jnp.dot(attn_rows, full_query, preferred_element_type=jnp.float32)
    keyval = jnp.dot(attn_rows, full_kv, preferred_element_type=jnp.float32)
    attended = attend(query, keyval, query_gain, key_gain, kv_count)
    attn_terms = project_out(attended, full_out)
    attn_part = attn_terms.astype(jnp.bfloat16).astype(jnp.float32)
    total = attn_part + moe_full
    summed = lax.psum(total, "tp")
    return (residual_in.astype(jnp.float32) + summed).astype(jnp.bfloat16)


def rotary_tables(length, width):
    half = width // 2
    position = jnp.arange(length, dtype=jnp.float32)
    freq = ROPE_BASE ** (-jnp.arange(half, dtype=jnp.float32) * 2.0 / width)
    angle = position[:, None] * freq[None, :]
    cosine, sine = jnp.cos(angle), jnp.sin(angle)
    return jnp.concatenate([cosine, cosine], 1), jnp.concatenate([-sine, sine], 1)


def spread_gates(moe_rows, router_weight, expert_ids):
    experts = router_weight.shape[0]
    logits = lax.dot_general(
        moe_rows, router_weight, (((1,), (1,)), ((), ())), preferred_element_type=jnp.float32
    )
    hits = jnp.any(
        expert_ids[:, :, None] == jnp.arange(experts, dtype=jnp.int32)[None, None, :], 1
    )
    scores = jnp.where(hits, jax.nn.sigmoid(logits), 0.0)
    return scores / jnp.sum(scores, 1, keepdims=True)


def rotated_norm(values, gain, cosine, sine):
    wide = values * lax.rsqrt(jnp.mean(values * values, -1, keepdims=True) + EPS) * gain
    return (wide * cosine + pltpu.roll(wide, HD // 2, 1) * sine).astype(jnp.bfloat16)


def attend_head(qkv, query_gain, key_gain, cosine, sine):
    seq = qkv.shape[0]
    query = rotated_norm(qkv[:, :HD], query_gain, cosine, sine)
    keys = rotated_norm(qkv[:, HD : 2 * HD], key_gain, cosine, sine)
    values = qkv[:, 2 * HD :].astype(jnp.bfloat16)
    logits = lax.dot_general(
        query, keys, (((1,), (1,)), ((), ())), preferred_element_type=jnp.float32
    ) * HD ** (-0.5)
    below = lax.broadcasted_iota(jnp.int32, (seq, seq), 0) >= lax.broadcasted_iota(
        jnp.int32, (seq, seq), 1
    )
    logits = jnp.where(below, logits, -1e30)
    expo = jnp.exp(logits - jnp.max(logits, -1, keepdims=True))
    probs = (expo / jnp.sum(expo, -1, keepdims=True)).astype(jnp.bfloat16)
    return jnp.dot(probs, values, preferred_element_type=jnp.float32).astype(jnp.bfloat16)


def half_expert(moe_ref, up_ref, down_ref):
    d_model = up_ref.shape[0]
    ff_dev = down_ref.shape[0]
    gates = moe_ref[:, d_model:].astype(jnp.float32)
    lane = lax.broadcasted_iota(jnp.int32, gates.shape, 1)
    gate = jnp.sum(jnp.where(lane == lax.axis_index("ep"), gates, 0.0), 1, keepdims=True)
    paired = jnp.dot(moe_ref[:, :d_model], up_ref[...], preferred_element_type=jnp.float32)
    front, back = paired[:, :ff_dev], paired[:, ff_dev:]
    hidden = (front / (1.0 + jnp.exp(-front)) * back * gate).astype(jnp.bfloat16)
    return jnp.dot(hidden, down_ref[...], preferred_element_type=jnp.float32)


def own_half(moe_ref, up_ref, down_ref, out_ref):
    out_ref[...] = half_expert(moe_ref, up_ref, down_ref)


def heads_and_half(
    seq, attn_ref, moe_ref, before_ref, qkv_ref, out_w_ref, up_ref, down_ref, qg_ref, kg_ref,
    cos_ref, sin_ref, out_ref,
):
    qkv = jnp.dot(attn_ref[...], qkv_ref[...], preferred_element_type=jnp.float32)
    parts = [
        jnp.concatenate(
            [
                attend_head(
                    qkv[at : at + seq, head : head + 3 * HD],
                    qg_ref[...], kg_ref[...], cos_ref[...], sin_ref[...],
                )
                for head in range(0, qkv.shape[1], 3 * HD)
            ],
            1,
        )
        for at in range(0, qkv.shape[0], seq)
    ]
    attended = jnp.concatenate(parts, 0)
    total = before_ref[...] + half_expert(moe_ref, up_ref, down_ref)
    total += jnp.dot(attended, out_w_ref[...], preferred_element_type=jnp.float32)
    out_ref[...] = total.astype(out_ref.dtype)


def rows_first(
    residual_in,
    shortcut,
    attn_gain,
    moe_gain,
    query_weight,
    key_value,
    output_weight,
    query_gain,
    key_gain,
    router_weight,
    expert_ids,
    gate_up_weight,
    down_weight,
):
    n_ep = lax.axis_size("ep")
    n_tp = lax.axis_size("tp")
    me, rank = lax.axis_index("ep"), lax.axis_index("tp")
    side = me % 2
    rows, d_model = residual_in.shape
    share = rows // 2
    depth = key_value.shape[0]
    their_up = from_partner(gate_up_weight, "tp", 0)
    their_down = from_partner(down_weight, "tp", 0)

    attn_rows = norm_rows(residual_in, attn_gain).astype(jnp.bfloat16)
    moe_rows = norm_rows(shortcut, moe_gain).astype(jnp.bfloat16)
    gates = spread_gates(moe_rows, router_weight, expert_ids).astype(jnp.bfloat16)
    gates = jnp.pad(gates, ((0, 0), (0, HD - gates.shape[1])))
    joined = jnp.concatenate([moe_rows, gates, attn_rows], 1)
    away = lax.dynamic_slice_in_dim(joined, (1 - side) * share, share, 0)
    kept = lax.dynamic_slice_in_dim(joined, side * share, share, 0)
    givers = [(at * n_tp + at % 2, (at ^ 1) * n_tp + at % 2) for at in range(n_ep)]
    given = lax.ppermute(away, ("ep", "tp"), givers)
    piece = jnp.where(side == rank, kept, given)
    all_moe = lax.all_gather(piece[:, : d_model + HD], "ep", axis=0, tiled=True)
    all_attn = lax.all_gather(piece[:, d_model + HD :], "ep", axis=0, tiled=True)

    kv_count = KVH // n_tp
    kv = lax.dynamic_slice_in_dim(
        key_value.reshape(depth, 2, KVH, HD), rank * kv_count, kv_count, 2
    )
    kv = jnp.repeat(kv, n_ep // kv_count, 2).transpose(0, 2, 1, 3).reshape(depth, n_ep, 2 * HD)
    sent = jnp.concatenate(
        [query_weight.reshape(depth, n_ep, HD), kv, output_weight.reshape(depth, n_ep, HD)], 2
    )
    mine = lax.all_to_all(sent, "ep", split_axis=1, concat_axis=0, tiled=True)
    mine = mine.reshape(d_model, 4 * HD)
    theirs = from_partner(mine, "tp", 0)
    qkv = jnp.concatenate([mine[:, : 3 * HD], theirs[:, : 3 * HD]], 1)
    out_w = jnp.concatenate([mine[:, 3 * HD :], theirs[:, 3 * HD :]], 1).T

    cosine, sine = rotary_tables(rows, HD)
    block = 2 * rows
    whole = lambda *shape: pl.BlockSpec(shape, lambda i: (0,) * len(shape))
    tiles = lambda width: pl.BlockSpec((block, width), lambda i: (i, 0))
    ff_dev = down_weight.shape[1]
    total = n_ep * share
    expert_flops = 6 * total * d_model * ff_dev
    params = pltpu.CompilerParams(vmem_limit_bytes=56 * 2**20)
    before = pl.pallas_call(
        own_half,
        grid=(total // block,),
        in_specs=[tiles(d_model + HD), whole(d_model, 2 * ff_dev), whole(ff_dev, d_model)],
        out_specs=tiles(d_model),
        out_shape=jax.ShapeDtypeStruct((total, d_model), jnp.float32),
        compiler_params=params,
        cost_estimate=pl.CostEstimate(
            flops=expert_flops,
            bytes_accessed=total * d_model * 6 + 3 * ff_dev * d_model * 2,
            transcendentals=total * ff_dev,
        ),
    )(all_moe, gate_up_weight[0], down_weight[0])
    partial_sum = pl.pallas_call(
        lambda *refs: heads_and_half(rows, *refs),
        grid=(total // block,),
        in_specs=[
            tiles(d_model),
            tiles(d_model + HD),
            tiles(d_model),
            whole(d_model, 6 * HD),
            whole(2 * HD, d_model),
            whole(d_model, 2 * ff_dev),
            whole(ff_dev, d_model),
            whole(1, HD),
            whole(1, HD),
            whole(rows, HD),
            whole(rows, HD),
        ],
        out_specs=tiles(d_model),
        out_shape=jax.ShapeDtypeStruct((total, d_model), jnp.bfloat16),
        compiler_params=params,
        cost_estimate=pl.CostEstimate(
            flops=expert_flops + 16 * total * d_model * HD,
            bytes_accessed=total * d_model * 10 + 3 * ff_dev * d_model * 2,
            transcendentals=total * ff_dev,
        ),
    )(
        all_attn, all_moe, before, qkv, out_w, their_up[0], their_down[0],
        query_gain[None], key_gain[None], cosine, sine,
    )
    summed = lax.psum_scatter(partial_sum, "ep", scatter_dimension=0, tiled=True)
    across = lax.ppermute(summed, "ep", [(at, at ^ 1) for at in range(n_ep)])
    low = jnp.where(side == 0, summed, across)
    high = jnp.where(side == 0, across, summed)
    sequence = jnp.concatenate([low, high], 0)
    owners = [(at * n_tp + at % 2, at * n_tp + 1 - at % 2) for at in range(n_ep)]
    handed = lax.ppermute(sequence, ("ep", "tp"), owners)
    summed = jnp.where(side == rank, sequence, handed)
    return (residual_in.astype(jnp.float32) + summed.astype(jnp.float32)).astype(jnp.bfloat16)


def solution(mesh):
    n_ep, n_tp = mesh.shape["ep"], mesh.shape["tp"]
    local = rows_first if n_ep * n_tp == QH and n_tp == 2 else weights_first
    return jax.shard_map(
        local,
        mesh=mesh,
        in_specs=(
            P("ep", None),
            P("ep", None),
            P(),
            P(),
            P("ep", "tp"),
            P("ep", None),
            P("ep", "tp"),
            P(),
            P(),
            P(),
            P("ep", None),
            P(("ep", "tp"), None, None),
            P(("ep", "tp"), None, None),
        ),
        out_specs=P("ep", None),
        check_vma=False,
    )
```

```python
import jax
import jax.numpy as jnp
from jax.experimental import pallas as pl
from jax.experimental.pallas import tpu as pltpu
from jax import lax
from jax.sharding import PartitionSpec as P

HD = 128
QH = 32
KVH = 4
TOPK = 8


EPS = 1e-06
ROPE_BASE = 1000000.0


def from_partner(value, axis, apart):
    mask = 2**apart
    pairs = [(source, source ^ mask) for source in range(lax.axis_size(axis))]
    return lax.ppermute(value, axis, pairs)


def norm_rows(values, gain):
    wide = values.astype(jnp.float32)
    return wide * lax.rsqrt(jnp.mean(wide * wide, -1, keepdims=True) + EPS) * gain


def rotary(values):
    length = values.shape[0]
    half = values.shape[-1] // 2
    position = jnp.arange(length, dtype=jnp.float32)
    freq = ROPE_BASE ** (-jnp.arange(half, dtype=jnp.float32) * 2.0 / values.shape[-1])
    angle = position[:, None] * freq[None, :]
    cosine = jnp.cos(angle)[:, None, :]
    sine = jnp.sin(angle)[:, None, :]
    first = values[..., :half]
    second = values[..., half:]
    return jnp.concatenate([first * cosine - second * sine, second * cosine + first * sine], -1)


def capacity_of(rows, experts):
    return max(2, 5 * rows * TOPK // (4 * experts))


def attend(query, keyval, query_gain, key_gain, kv_count):
    seq = query.shape[0]
    query = rotary(norm_rows(query.reshape(seq, -1, HD), query_gain)).astype(jnp.bfloat16)
    heads = query.shape[1]
    query = query.reshape(seq, kv_count, heads // kv_count, HD)
    keyval = keyval.reshape(seq, 2, kv_count, HD)
    keys = rotary(norm_rows(keyval[:, 0], key_gain)).astype(jnp.bfloat16)
    values = keyval[:, 1].astype(jnp.bfloat16)
    logits = jnp.einsum("sgjd,tgd->gjst", query, keys, preferred_element_type=jnp.float32) * HD ** (
        -0.5
    )
    causal = jnp.arange(seq)[:, None] >= jnp.arange(seq)[None, :]
    logits = jnp.where(causal, logits, -1e30)
    peak = jnp.max(logits, -1, keepdims=True)
    expo = jnp.exp(logits - peak)
    probs = (expo / jnp.sum(expo, -1, keepdims=True)).astype(jnp.bfloat16)
    attended = jnp.einsum("gjst,tgd->sgjd", probs, values, preferred_element_type=jnp.float32)
    return attended.astype(jnp.bfloat16).reshape(seq, heads * HD)


def project_out(attended, weight):
    return lax.dot_general(
        attended, weight, (((1,), (1,)), ((), ())), preferred_element_type=jnp.float32
    )


def weights_first(
    residual_in,
    shortcut,
    attn_gain,
    moe_gain,
    query_weight,
    key_value,
    output_weight,
    query_gain,
    key_gain,
    router_weight,
    expert_ids,
    gate_up_weight,
    down_weight,
):
    n_ep = lax.axis_size("ep")
    n_tp = lax.axis_size("tp")
    rank = lax.axis_index("tp")
    pairs = n_tp // 2
    group_id = rank // 2
    side = rank % 2
    rows, d_model = residual_in.shape
    half_width = d_model // 2
    experts = router_weight.shape[0]
    capacity = capacity_of(rows, experts)
    ff_dev = down_weight.shape[1]
    qh_dev = query_weight.shape[1] // HD
    group = QH // KVH
    kv_count = max(1, qh_dev // group)
    kv_start = rank * qh_dev // group
    attn_rows = norm_rows(residual_in, attn_gain).astype(jnp.bfloat16)
    moe_rows = norm_rows(shortcut, moe_gain).astype(jnp.bfloat16)
    logits_router = lax.dot_general(
        moe_rows, router_weight, (((1,), (1,)), ((), ())), preferred_element_type=jnp.float32
    )
    hits = (expert_ids[:, :, None] == jnp.arange(experts, dtype=jnp.int32)[None, None, :]).astype(
        jnp.float32
    )
    chosen = jnp.sum(hits * logits_router[:, None, :], -1)
    scores = jax.nn.sigmoid(chosen)
    gates = (scores / jnp.sum(scores, 1, keepdims=True)).astype(jnp.bfloat16)
    per_row = jnp.sum(hits, 1).astype(jnp.bfloat16)
    lower = (jnp.arange(rows)[:, None] > jnp.arange(rows)[None, :]).astype(jnp.bfloat16)
    earlier = jnp.dot(lower, per_row, preferred_element_type=jnp.float32)
    slot = jnp.sum(hits * earlier[:, None, :], -1)
    mine = expert_ids % pairs == group_id
    target = (expert_ids // pairs).astype(jnp.float32) * capacity + slot
    target = jnp.where(mine, target, -1.0)
    places = jnp.arange(n_ep * capacity, dtype=jnp.float32)
    match = (target[:, :, None] == places[None, None, :]).astype(jnp.float32)
    dispatch_map = jnp.sum(match, 1).astype(jnp.bfloat16)
    combine = jnp.sum(match * gates.astype(jnp.float32)[:, :, None], 1).astype(jnp.bfloat16)
    outgoing = lax.dot_general(
        dispatch_map, moe_rows, (((0,), (0,)), ((), ())), preferred_element_type=jnp.float32
    ).astype(jnp.bfloat16)
    outgoing = outgoing.reshape(n_ep, capacity, d_model)
    arrived = lax.all_to_all(outgoing, "ep", split_axis=0, concat_axis=0, tiled=True)
    paired = jnp.einsum(
        "ack,kf->acf", arrived, gate_up_weight[0], preferred_element_type=jnp.float32
    )
    hidden = (jax.nn.silu(paired[..., :ff_dev]) * paired[..., ff_dev:]).astype(jnp.bfloat16)
    partial_sum = jnp.einsum(
        "acf,fk->ack", hidden, down_weight[0], preferred_element_type=jnp.float32
    )
    kept = lax.dynamic_slice_in_dim(partial_sum, side * half_width, half_width, 2)
    handed = lax.dynamic_slice_in_dim(partial_sum, (1 - side) * half_width, half_width, 2)
    received = from_partner(handed.astype(jnp.bfloat16), "tp", 0).astype(handed.dtype)
    expert_out = (kept + received).astype(jnp.bfloat16)
    returned = lax.all_to_all(expert_out, "ep", split_axis=0, concat_axis=0, tiled=True).reshape(
        -1, half_width
    )
    moe_cols = jnp.dot(combine, returned, preferred_element_type=jnp.float32)
    blank = jnp.zeros_like(moe_cols)
    moe_full = jnp.where(
        side == 0, jnp.concatenate([moe_cols, blank], 1), jnp.concatenate([blank, moe_cols], 1)
    )
    local_rows = key_value.shape[0]
    local_kv = lax.dynamic_slice_in_dim(
        key_value.reshape(local_rows, 2, KVH, HD), kv_start, kv_count, 2
    )
    local_kv = local_kv.reshape(local_rows, 2 * kv_count * HD)
    full_query, full_kv, full_out = (
        lax.all_gather(query_weight, "ep", axis=0, tiled=True),
        lax.all_gather(local_kv, "ep", axis=0, tiled=True),
        lax.all_gather(output_weight, "ep", axis=0, tiled=True),
    )
    query = jnp.dot(attn_rows, full_query, preferred_element_type=jnp.float32)
    keyval = jnp.dot(attn_rows, full_kv, preferred_element_type=jnp.float32)
    attended = attend(query, keyval, query_gain, key_gain, kv_count)
    attn_terms = project_out(attended, full_out)
    attn_part = attn_terms.astype(jnp.bfloat16).astype(jnp.float32)
    total = attn_part + moe_full
    summed = lax.psum(total, "tp")
    return (residual_in.astype(jnp.float32) + summed).astype(jnp.bfloat16)


def rotary_tables(length, width):
    half = width // 2
    position = jnp.arange(length, dtype=jnp.float32)
    freq = ROPE_BASE ** (-jnp.arange(half, dtype=jnp.float32) * 2.0 / width)
    angle = position[:, None] * freq[None, :]
    cosine, sine = jnp.cos(angle), jnp.sin(angle)
    return jnp.concatenate([cosine, cosine], 1), jnp.concatenate([-sine, sine], 1)


def spread_gates(moe_rows, router_weight, expert_ids):
    experts = router_weight.shape[0]
    logits = lax.dot_general(
        moe_rows, router_weight, (((1,), (1,)), ((), ())), preferred_element_type=jnp.float32
    )
    hits = jnp.any(
        expert_ids[:, :, None] == jnp.arange(experts, dtype=jnp.int32)[None, None, :], 1
    )
    scores = jnp.where(hits, jax.nn.sigmoid(logits), 0.0)
    return scores / jnp.sum(scores, 1, keepdims=True)


def rotated_norm(values, gain, cosine, sine):
    wide = values * lax.rsqrt(jnp.mean(values * values, -1, keepdims=True) + EPS) * gain
    return (wide * cosine + pltpu.roll(wide, HD // 2, 1) * sine).astype(jnp.bfloat16)


def attend_head(qkv, query_gain, key_gain, cosine, sine):
    seq = qkv.shape[0]
    query = rotated_norm(qkv[:, :HD], query_gain, cosine, sine)
    keys = rotated_norm(qkv[:, HD : 2 * HD], key_gain, cosine, sine)
    values = qkv[:, 2 * HD :].astype(jnp.bfloat16)
    logits = lax.dot_general(
        query, keys, (((1,), (1,)), ((), ())), preferred_element_type=jnp.float32
    ) * HD ** (-0.5)
    below = lax.broadcasted_iota(jnp.int32, (seq, seq), 0) >= lax.broadcasted_iota(
        jnp.int32, (seq, seq), 1
    )
    logits = jnp.where(below, logits, -1e30)
    expo = jnp.exp(logits - jnp.max(logits, -1, keepdims=True))
    probs = (expo / jnp.sum(expo, -1, keepdims=True)).astype(jnp.bfloat16)
    return jnp.dot(probs, values, preferred_element_type=jnp.float32).astype(jnp.bfloat16)


def half_expert(moe_ref, up_ref, down_ref):
    d_model = up_ref.shape[0]
    ff_dev = down_ref.shape[0]
    gates = moe_ref[:, d_model:].astype(jnp.float32)
    lane = lax.broadcasted_iota(jnp.int32, gates.shape, 1)
    gate = jnp.sum(jnp.where(lane == lax.axis_index("ep"), gates, 0.0), 1, keepdims=True)
    paired = jnp.dot(moe_ref[:, :d_model], up_ref[...], preferred_element_type=jnp.float32)
    front, back = paired[:, :ff_dev], paired[:, ff_dev:]
    hidden = (front / (1.0 + jnp.exp(-front)) * back * gate).astype(jnp.bfloat16)
    return jnp.dot(hidden, down_ref[...], preferred_element_type=jnp.float32)


def own_half(moe_ref, up_ref, down_ref, out_ref):
    out_ref[...] = half_expert(moe_ref, up_ref, down_ref)


def other_half(moe_ref, before_ref, up_ref, down_ref, out_ref):
    total = before_ref[...] + half_expert(moe_ref, up_ref, down_ref)
    out_ref[...] = total.astype(out_ref.dtype)


def two_heads(
    seq, attn_ref, before_ref, qkv_ref, out_w_ref, qg_ref, kg_ref, cos_ref, sin_ref, out_ref
):
    qkv = jnp.dot(attn_ref[...], qkv_ref[...], preferred_element_type=jnp.float32)
    parts = [
        jnp.concatenate(
            [
                attend_head(
                    qkv[at : at + seq, head : head + 3 * HD],
                    qg_ref[...], kg_ref[...], cos_ref[...], sin_ref[...],
                )
                for head in range(0, qkv.shape[1], 3 * HD)
            ],
            1,
        )
        for at in range(0, qkv.shape[0], seq)
    ]
    attended = jnp.concatenate(parts, 0)
    out_ref[...] = before_ref[...] + jnp.dot(
        attended, out_w_ref[...], preferred_element_type=jnp.float32
    )


def rows_first(
    residual_in,
    shortcut,
    attn_gain,
    moe_gain,
    query_weight,
    key_value,
    output_weight,
    query_gain,
    key_gain,
    router_weight,
    expert_ids,
    gate_up_weight,
    down_weight,
):
    n_ep = lax.axis_size("ep")
    n_tp = lax.axis_size("tp")
    me, rank = lax.axis_index("ep"), lax.axis_index("tp")
    side = me % 2
    rows, d_model = residual_in.shape
    share = rows // 2
    depth = key_value.shape[0]
    their_up = from_partner(gate_up_weight, "tp", 0)
    their_down = from_partner(down_weight, "tp", 0)

    attn_rows = norm_rows(residual_in, attn_gain).astype(jnp.bfloat16)
    moe_rows = norm_rows(shortcut, moe_gain).astype(jnp.bfloat16)
    gates = spread_gates(moe_rows, router_weight, expert_ids).astype(jnp.bfloat16)
    gates = jnp.pad(gates, ((0, 0), (0, HD - gates.shape[1])))
    joined = jnp.concatenate([moe_rows, gates, attn_rows], 1)
    away = lax.dynamic_slice_in_dim(joined, (1 - side) * share, share, 0)
    kept = lax.dynamic_slice_in_dim(joined, side * share, share, 0)
    givers = [(at * n_tp + at % 2, (at ^ 1) * n_tp + at % 2) for at in range(n_ep)]
    given = lax.ppermute(away, ("ep", "tp"), givers)
    piece = jnp.where(side == rank, kept, given)
    all_moe = lax.all_gather(piece[:, : d_model + HD], "ep", axis=0, tiled=True)
    all_attn = lax.all_gather(piece[:, d_model + HD :], "ep", axis=0, tiled=True)

    kv_count = KVH // n_tp
    pairs = key_value.reshape(depth, 2, n_tp, kv_count, HD)
    kv = jnp.where(rank == 0, pairs, pairs[:, :, ::-1]).transpose(0, 3, 2, 1, 4)
    kv = jnp.repeat(kv.reshape(depth, kv_count, 4 * HD), n_ep // kv_count, 1)
    sent = jnp.concatenate(
        [query_weight.reshape(depth, n_ep, HD), output_weight.reshape(depth, n_ep, HD), kv], 2
    )
    mine = lax.all_to_all(sent, "ep", split_axis=1, concat_axis=0, tiled=True)
    mine = mine.reshape(d_model, 6 * HD)
    theirs = from_partner(mine[:, : 2 * HD], "tp", 0)

    cosine, sine = rotary_tables(rows, HD)
    block = 2 * rows
    whole = lambda *shape: pl.BlockSpec(shape, lambda i: (0,) * len(shape))
    tiles = lambda width: pl.BlockSpec((block, width), lambda i: (i, 0))
    ff_dev = down_weight.shape[1]
    total = n_ep * share
    expert_flops = 6 * total * d_model * ff_dev
    params = pltpu.CompilerParams(vmem_limit_bytes=56 * 2**20)
    before = pl.pallas_call(
        own_half,
        grid=(total // block,),
        in_specs=[tiles(d_model + HD), whole(d_model, 2 * ff_dev), whole(ff_dev, d_model)],
        out_specs=tiles(d_model),
        out_shape=jax.ShapeDtypeStruct((total, d_model), jnp.float32),
        compiler_params=params,
        cost_estimate=pl.CostEstimate(
            flops=expert_flops,
            bytes_accessed=total * d_model * 6 + 3 * ff_dev * d_model * 2,
            transcendentals=total * ff_dev,
        ),
    )(all_moe, gate_up_weight[0], down_weight[0])
    theirs, before = lax.optimization_barrier((theirs, before))
    qkv = jnp.concatenate(
        [mine[:, :HD], mine[:, 2 * HD : 4 * HD], theirs[:, :HD], mine[:, 4 * HD :]], 1
    )
    out_w = jnp.concatenate([mine[:, HD : 2 * HD], theirs[:, HD:]], 1).T
    before = pl.pallas_call(
        lambda *refs: two_heads(rows, *refs),
        grid=(total // block,),
        in_specs=[
            tiles(d_model),
            tiles(d_model),
            whole(d_model, 6 * HD),
            whole(2 * HD, d_model),
            whole(1, HD),
            whole(1, HD),
            whole(rows, HD),
            whole(rows, HD),
        ],
        out_specs=tiles(d_model),
        out_shape=jax.ShapeDtypeStruct((total, d_model), jnp.float32),
        compiler_params=params,
        cost_estimate=pl.CostEstimate(
            flops=16 * total * d_model * HD,
            bytes_accessed=total * d_model * 10 + 8 * HD * d_model * 2,
            transcendentals=total * rows * 2,
        ),
    )(
        all_attn, before, qkv, out_w, query_gain[None], key_gain[None], cosine, sine,
    )
    their_up, their_down, before = lax.optimization_barrier((their_up, their_down, before))
    partial_sum = pl.pallas_call(
        other_half,
        grid=(total // block,),
        in_specs=[
            tiles(d_model + HD),
            tiles(d_model),
            whole(d_model, 2 * ff_dev),
            whole(ff_dev, d_model),
        ],
        out_specs=tiles(d_model),
        out_shape=jax.ShapeDtypeStruct((total, d_model), jnp.bfloat16),
        compiler_params=params,
        cost_estimate=pl.CostEstimate(
            flops=expert_flops,
            bytes_accessed=total * d_model * 8 + 3 * ff_dev * d_model * 2,
            transcendentals=total * ff_dev,
        ),
    )(all_moe, before, their_up[0], their_down[0])
    summed = lax.psum_scatter(partial_sum, "ep", scatter_dimension=0, tiled=True)
    across = lax.ppermute(summed, "ep", [(at, at ^ 1) for at in range(n_ep)])
    low = jnp.where(side == 0, summed, across)
    high = jnp.where(side == 0, across, summed)
    sequence = jnp.concatenate([low, high], 0)
    owners = [(at * n_tp + at % 2, at * n_tp + 1 - at % 2) for at in range(n_ep)]
    handed = lax.ppermute(sequence, ("ep", "tp"), owners)
    summed = jnp.where(side == rank, sequence, handed)
    return (residual_in.astype(jnp.float32) + summed.astype(jnp.float32)).astype(jnp.bfloat16)


def solution(mesh):
    n_ep, n_tp = mesh.shape["ep"], mesh.shape["tp"]
    local = rows_first if n_ep * n_tp == QH and n_tp == 2 else weights_first
    return jax.shard_map(
        local,
        mesh=mesh,
        in_specs=(
            P("ep", None),
            P("ep", None),
            P(),
            P(),
            P("ep", "tp"),
            P("ep", None),
            P("ep", "tp"),
            P(),
            P(),
            P(),
            P("ep", None),
            P(("ep", "tp"), None, None),
            P(("ep", "tp"), None, None),
        ),
        out_specs=P("ep", None),
        check_vma=False,
    )
```

```python
import jax
import jax.numpy as jnp
from jax.experimental import pallas as pl
from jax.experimental.pallas import tpu as pltpu
from jax import lax
from jax.sharding import PartitionSpec as P

HD = 128
QH = 32
KVH = 4
TOPK = 8


EPS = 1e-06
ROPE_BASE = 1000000.0


def from_partner(value, axis, apart):
    mask = 2**apart
    pairs = [(source, source ^ mask) for source in range(lax.axis_size(axis))]
    return lax.ppermute(value, axis, pairs)


def norm_rows(values, gain):
    wide = values.astype(jnp.float32)
    return wide * lax.rsqrt(jnp.mean(wide * wide, -1, keepdims=True) + EPS) * gain


def rotary(values):
    length = values.shape[0]
    half = values.shape[-1] // 2
    position = jnp.arange(length, dtype=jnp.float32)
    freq = ROPE_BASE ** (-jnp.arange(half, dtype=jnp.float32) * 2.0 / values.shape[-1])
    angle = position[:, None] * freq[None, :]
    cosine = jnp.cos(angle)[:, None, :]
    sine = jnp.sin(angle)[:, None, :]
    first = values[..., :half]
    second = values[..., half:]
    return jnp.concatenate([first * cosine - second * sine, second * cosine + first * sine], -1)


def capacity_of(rows, experts):
    return max(2, 5 * rows * TOPK // (4 * experts))


def attend(query, keyval, query_gain, key_gain, kv_count):
    seq = query.shape[0]
    query = rotary(norm_rows(query.reshape(seq, -1, HD), query_gain)).astype(jnp.bfloat16)
    heads = query.shape[1]
    query = query.reshape(seq, kv_count, heads // kv_count, HD)
    keyval = keyval.reshape(seq, 2, kv_count, HD)
    keys = rotary(norm_rows(keyval[:, 0], key_gain)).astype(jnp.bfloat16)
    values = keyval[:, 1].astype(jnp.bfloat16)
    logits = jnp.einsum("sgjd,tgd->gjst", query, keys, preferred_element_type=jnp.float32) * HD ** (
        -0.5
    )
    causal = jnp.arange(seq)[:, None] >= jnp.arange(seq)[None, :]
    logits = jnp.where(causal, logits, -1e30)
    peak = jnp.max(logits, -1, keepdims=True)
    expo = jnp.exp(logits - peak)
    probs = (expo / jnp.sum(expo, -1, keepdims=True)).astype(jnp.bfloat16)
    attended = jnp.einsum("gjst,tgd->sgjd", probs, values, preferred_element_type=jnp.float32)
    return attended.astype(jnp.bfloat16).reshape(seq, heads * HD)


def project_out(attended, weight):
    return lax.dot_general(
        attended, weight, (((1,), (1,)), ((), ())), preferred_element_type=jnp.float32
    )


def weights_first(
    residual_in,
    shortcut,
    attn_gain,
    moe_gain,
    query_weight,
    key_value,
    output_weight,
    query_gain,
    key_gain,
    router_weight,
    expert_ids,
    gate_up_weight,
    down_weight,
):
    n_ep = lax.axis_size("ep")
    n_tp = lax.axis_size("tp")
    rank = lax.axis_index("tp")
    pairs = n_tp // 2
    group_id = rank // 2
    side = rank % 2
    rows, d_model = residual_in.shape
    half_width = d_model // 2
    experts = router_weight.shape[0]
    capacity = capacity_of(rows, experts)
    ff_dev = down_weight.shape[1]
    qh_dev = query_weight.shape[1] // HD
    group = QH // KVH
    kv_count = max(1, qh_dev // group)
    kv_start = rank * qh_dev // group
    attn_rows = norm_rows(residual_in, attn_gain).astype(jnp.bfloat16)
    moe_rows = norm_rows(shortcut, moe_gain).astype(jnp.bfloat16)
    logits_router = lax.dot_general(
        moe_rows, router_weight, (((1,), (1,)), ((), ())), preferred_element_type=jnp.float32
    )
    hits = (expert_ids[:, :, None] == jnp.arange(experts, dtype=jnp.int32)[None, None, :]).astype(
        jnp.float32
    )
    chosen = jnp.sum(hits * logits_router[:, None, :], -1)
    scores = jax.nn.sigmoid(chosen)
    gates = (scores / jnp.sum(scores, 1, keepdims=True)).astype(jnp.bfloat16)
    per_row = jnp.sum(hits, 1).astype(jnp.bfloat16)
    lower = (jnp.arange(rows)[:, None] > jnp.arange(rows)[None, :]).astype(jnp.bfloat16)
    earlier = jnp.dot(lower, per_row, preferred_element_type=jnp.float32)
    slot = jnp.sum(hits * earlier[:, None, :], -1)
    mine = expert_ids % pairs == group_id
    target = (expert_ids // pairs).astype(jnp.float32) * capacity + slot
    target = jnp.where(mine, target, -1.0)
    places = jnp.arange(n_ep * capacity, dtype=jnp.float32)
    match = (target[:, :, None] == places[None, None, :]).astype(jnp.float32)
    dispatch_map = jnp.sum(match, 1).astype(jnp.bfloat16)
    combine = jnp.sum(match * gates.astype(jnp.float32)[:, :, None], 1).astype(jnp.bfloat16)
    outgoing = lax.dot_general(
        dispatch_map, moe_rows, (((0,), (0,)), ((), ())), preferred_element_type=jnp.float32
    ).astype(jnp.bfloat16)
    outgoing = outgoing.reshape(n_ep, capacity, d_model)
    arrived = lax.all_to_all(outgoing, "ep", split_axis=0, concat_axis=0, tiled=True)
    paired = jnp.einsum(
        "ack,kf->acf", arrived, gate_up_weight[0], preferred_element_type=jnp.float32
    )
    hidden = (jax.nn.silu(paired[..., :ff_dev]) * paired[..., ff_dev:]).astype(jnp.bfloat16)
    partial_sum = jnp.einsum(
        "acf,fk->ack", hidden, down_weight[0], preferred_element_type=jnp.float32
    )
    kept = lax.dynamic_slice_in_dim(partial_sum, side * half_width, half_width, 2)
    handed = lax.dynamic_slice_in_dim(partial_sum, (1 - side) * half_width, half_width, 2)
    received = from_partner(handed.astype(jnp.bfloat16), "tp", 0).astype(handed.dtype)
    expert_out = (kept + received).astype(jnp.bfloat16)
    returned = lax.all_to_all(expert_out, "ep", split_axis=0, concat_axis=0, tiled=True).reshape(
        -1, half_width
    )
    moe_cols = jnp.dot(combine, returned, preferred_element_type=jnp.float32)
    blank = jnp.zeros_like(moe_cols)
    moe_full = jnp.where(
        side == 0, jnp.concatenate([moe_cols, blank], 1), jnp.concatenate([blank, moe_cols], 1)
    )
    local_rows = key_value.shape[0]
    local_kv = lax.dynamic_slice_in_dim(
        key_value.reshape(local_rows, 2, KVH, HD), kv_start, kv_count, 2
    )
    local_kv = local_kv.reshape(local_rows, 2 * kv_count * HD)
    full_query, full_kv, full_out = (
        lax.all_gather(query_weight, "ep", axis=0, tiled=True),
        lax.all_gather(local_kv, "ep", axis=0, tiled=True),
        lax.all_gather(output_weight, "ep", axis=0, tiled=True),
    )
    query = jnp.dot(attn_rows, full_query, preferred_element_type=jnp.float32)
    keyval = jnp.dot(attn_rows, full_kv, preferred_element_type=jnp.float32)
    attended = attend(query, keyval, query_gain, key_gain, kv_count)
    attn_terms = project_out(attended, full_out)
    attn_part = attn_terms.astype(jnp.bfloat16).astype(jnp.float32)
    total = attn_part + moe_full
    summed = lax.psum(total, "tp")
    return (residual_in.astype(jnp.float32) + summed).astype(jnp.bfloat16)


def rotary_tables(length, width):
    half = width // 2
    position = jnp.arange(length, dtype=jnp.float32)
    freq = ROPE_BASE ** (-jnp.arange(half, dtype=jnp.float32) * 2.0 / width)
    angle = position[:, None] * freq[None, :]
    cosine, sine = jnp.cos(angle), jnp.sin(angle)
    return jnp.concatenate([cosine, cosine], 1), jnp.concatenate([-sine, sine], 1)


def spread_gates(moe_rows, router_weight, expert_ids):
    experts = router_weight.shape[0]
    logits = lax.dot_general(
        moe_rows, router_weight, (((1,), (1,)), ((), ())), preferred_element_type=jnp.float32
    )
    hits = jnp.any(
        expert_ids[:, :, None] == jnp.arange(experts, dtype=jnp.int32)[None, None, :], 1
    )
    scores = jnp.where(hits, jax.nn.sigmoid(logits), 0.0)
    return scores / jnp.sum(scores, 1, keepdims=True)


def rotated_norm(values, gain, cosine, sine):
    wide = values * lax.rsqrt(jnp.mean(values * values, -1, keepdims=True) + EPS) * gain
    return (wide * cosine + pltpu.roll(wide, HD // 2, 1) * sine).astype(jnp.bfloat16)


def attend_head(qkv, query_gain, key_gain, cosine, sine):
    seq = qkv.shape[0]
    query = rotated_norm(qkv[:, :HD], query_gain, cosine, sine)
    keys = rotated_norm(qkv[:, HD : 2 * HD], key_gain, cosine, sine)
    values = qkv[:, 2 * HD :].astype(jnp.bfloat16)
    logits = lax.dot_general(
        query, keys, (((1,), (1,)), ((), ())), preferred_element_type=jnp.float32
    ) * HD ** (-0.5)
    below = lax.broadcasted_iota(jnp.int32, (seq, seq), 0) >= lax.broadcasted_iota(
        jnp.int32, (seq, seq), 1
    )
    logits = jnp.where(below, logits, -1e30)
    expo = jnp.exp(logits - jnp.max(logits, -1, keepdims=True))
    probs = (expo / jnp.sum(expo, -1, keepdims=True)).astype(jnp.bfloat16)
    return jnp.dot(probs, values, preferred_element_type=jnp.float32).astype(jnp.bfloat16)


def half_expert(moe_ref, up_ref, down_ref):
    d_model = up_ref.shape[0]
    ff_dev = down_ref.shape[0]
    gates = moe_ref[:, d_model:].astype(jnp.float32)
    lane = lax.broadcasted_iota(jnp.int32, gates.shape, 1)
    gate = jnp.sum(jnp.where(lane == lax.axis_index("ep"), gates, 0.0), 1, keepdims=True)
    paired = jnp.dot(moe_ref[:, :d_model], up_ref[...], preferred_element_type=jnp.float32)
    front, back = paired[:, :ff_dev], paired[:, ff_dev:]
    hidden = (front / (1.0 + jnp.exp(-front)) * back * gate).astype(jnp.bfloat16)
    return jnp.dot(hidden, down_ref[...], preferred_element_type=jnp.float32)


def own_half(moe_ref, up_ref, down_ref, out_ref):
    out_ref[...] = half_expert(moe_ref, up_ref, down_ref)


def other_half(moe_ref, before_ref, up_ref, down_ref, out_ref):
    total = before_ref[...] + half_expert(moe_ref, up_ref, down_ref)
    out_ref[...] = total.astype(out_ref.dtype)


def two_heads(
    seq, attn_ref, before_ref, qkv_ref, out_w_ref, qg_ref, kg_ref, cos_ref, sin_ref, out_ref
):
    qkv = jnp.dot(attn_ref[...], qkv_ref[...], preferred_element_type=jnp.float32)
    parts = [
        jnp.concatenate(
            [
                attend_head(
                    jnp.concatenate(
                        [qkv[at : at + seq, head : head + HD], qkv[at : at + seq, 2 * HD :]], 1
                    ),
                    qg_ref[...], kg_ref[...], cos_ref[...], sin_ref[...],
                )
                for head in (0, HD)
            ],
            1,
        )
        for at in range(0, qkv.shape[0], seq)
    ]
    attended = jnp.concatenate(parts, 0)
    out_ref[...] = before_ref[...] + jnp.dot(
        attended, out_w_ref[...], preferred_element_type=jnp.float32
    )


def rows_first(
    residual_in,
    shortcut,
    attn_gain,
    moe_gain,
    query_weight,
    key_value,
    output_weight,
    query_gain,
    key_gain,
    router_weight,
    expert_ids,
    gate_up_weight,
    down_weight,
):
    n_ep = lax.axis_size("ep")
    n_tp = lax.axis_size("tp")
    me, rank = lax.axis_index("ep"), lax.axis_index("tp")
    side = me % 2
    rows, d_model = residual_in.shape
    share = rows // 2
    depth = key_value.shape[0]
    own_w = jnp.stack([query_weight, output_weight])
    their_w = from_partner(own_w, "tp", 0)
    their_up = from_partner(gate_up_weight, "tp", 0)
    their_down = from_partner(down_weight, "tp", 0)

    attn_rows = norm_rows(residual_in, attn_gain).astype(jnp.bfloat16)
    moe_rows = norm_rows(shortcut, moe_gain).astype(jnp.bfloat16)
    gates = spread_gates(moe_rows, router_weight, expert_ids).astype(jnp.bfloat16)
    gates = jnp.pad(gates, ((0, 0), (0, HD - gates.shape[1])))
    joined = jnp.concatenate([moe_rows, gates, attn_rows], 1)
    away = lax.dynamic_slice_in_dim(joined, (1 - side) * share, share, 0)
    kept = lax.dynamic_slice_in_dim(joined, side * share, share, 0)
    givers = [(at * n_tp + at % 2, (at ^ 1) * n_tp + at % 2) for at in range(n_ep)]
    given = lax.ppermute(away, ("ep", "tp"), givers)
    piece = jnp.where(side == rank, kept, given)
    all_moe = lax.all_gather(piece[:, : d_model + HD], "ep", axis=0, tiled=True)
    all_attn = lax.all_gather(piece[:, d_model + HD :], "ep", axis=0, tiled=True)

    kv = key_value.reshape(depth, 2, KVH, HD).transpose(0, 2, 1, 3)
    kv = jnp.repeat(kv.reshape(depth, KVH, 2 * HD), n_ep // KVH, 1)
    low = jnp.where(rank == 0, own_w, their_w)
    high = jnp.where(rank == 0, their_w, own_w)
    both = jnp.concatenate([low, high], 2).reshape(2, depth, n_ep, 2 * HD)
    sent = jnp.concatenate([both[0], both[1], kv], 2)
    mine = lax.all_to_all(sent, "ep", split_axis=1, concat_axis=0, tiled=True)
    mine = mine.reshape(d_model, 6 * HD)

    cosine, sine = rotary_tables(rows, HD)
    block = 2 * rows
    whole = lambda *shape: pl.BlockSpec(shape, lambda i: (0,) * len(shape))
    tiles = lambda width: pl.BlockSpec((block, width), lambda i: (i, 0))
    ff_dev = down_weight.shape[1]
    total = n_ep * share
    expert_flops = 6 * total * d_model * ff_dev
    params = pltpu.CompilerParams(vmem_limit_bytes=56 * 2**20)
    before = pl.pallas_call(
        own_half,
        grid=(total // block,),
        in_specs=[tiles(d_model + HD), whole(d_model, 2 * ff_dev), whole(ff_dev, d_model)],
        out_specs=tiles(d_model),
        out_shape=jax.ShapeDtypeStruct((total, d_model), jnp.float32),
        compiler_params=params,
        cost_estimate=pl.CostEstimate(
            flops=expert_flops,
            bytes_accessed=total * d_model * 6 + 3 * ff_dev * d_model * 2,
            transcendentals=total * ff_dev,
        ),
    )(all_moe, gate_up_weight[0], down_weight[0])
    qkv = jnp.concatenate([mine[:, : 2 * HD], mine[:, 4 * HD :]], 1)
    out_w = mine[:, 2 * HD : 4 * HD].T
    before = pl.pallas_call(
        lambda *refs: two_heads(rows, *refs),
        grid=(total // block,),
        in_specs=[
            tiles(d_model),
            tiles(d_model),
            whole(d_model, 4 * HD),
            whole(2 * HD, d_model),
            whole(1, HD),
            whole(1, HD),
            whole(rows, HD),
            whole(rows, HD),
        ],
        out_specs=tiles(d_model),
        out_shape=jax.ShapeDtypeStruct((total, d_model), jnp.float32),
        compiler_params=params,
        cost_estimate=pl.CostEstimate(
            flops=12 * total * d_model * HD,
            bytes_accessed=total * d_model * 10 + 8 * HD * d_model * 2,
            transcendentals=total * rows * 2,
        ),
    )(
        all_attn, before, qkv, out_w, query_gain[None], key_gain[None], cosine, sine,
    )
    their_up, their_down, before = lax.optimization_barrier((their_up, their_down, before))
    partial_sum = pl.pallas_call(
        other_half,
        grid=(total // block,),
        in_specs=[
            tiles(d_model + HD),
            tiles(d_model),
            whole(d_model, 2 * ff_dev),
            whole(ff_dev, d_model),
        ],
        out_specs=tiles(d_model),
        out_shape=jax.ShapeDtypeStruct((total, d_model), jnp.bfloat16),
        compiler_params=params,
        cost_estimate=pl.CostEstimate(
            flops=expert_flops,
            bytes_accessed=total * d_model * 8 + 3 * ff_dev * d_model * 2,
            transcendentals=total * ff_dev,
        ),
    )(all_moe, before, their_up[0], their_down[0])
    summed = lax.psum_scatter(partial_sum, "ep", scatter_dimension=0, tiled=True)
    across = lax.ppermute(summed, "ep", [(at, at ^ 1) for at in range(n_ep)])
    low = jnp.where(side == 0, summed, across)
    high = jnp.where(side == 0, across, summed)
    sequence = jnp.concatenate([low, high], 0)
    owners = [(at * n_tp + at % 2, at * n_tp + 1 - at % 2) for at in range(n_ep)]
    handed = lax.ppermute(sequence, ("ep", "tp"), owners)
    summed = jnp.where(side == rank, sequence, handed)
    return (residual_in.astype(jnp.float32) + summed.astype(jnp.float32)).astype(jnp.bfloat16)


def solution(mesh):
    n_ep, n_tp = mesh.shape["ep"], mesh.shape["tp"]
    local = rows_first if n_ep * n_tp == QH and n_tp == 2 else weights_first
    return jax.shard_map(
        local,
        mesh=mesh,
        in_specs=(
            P("ep", None),
            P("ep", None),
            P(),
            P(),
            P("ep", "tp"),
            P("ep", None),
            P("ep", "tp"),
            P(),
            P(),
            P(),
            P("ep", None),
            P(("ep", "tp"), None, None),
            P(("ep", "tp"), None, None),
        ),
        out_specs=P("ep", None),
        check_vma=False,
    )
```
